32 devices in a mesh: grp: 2 (over core), fsdp: 16 (over z, y, x).
Axes of the slice: x: 2, y: 2, z: 4, core: 2. Of those that a mesh axis runs over, the one named last changes fastest.
Arguments:
- scorer_hidden: bfloat16 [4096, 4096], P(('grp', 'fsdp')), may hold values from -6 to 6
- scorer_gain: float32 [4096], replicated, may hold values from 0.3 to 40
- scorer_head: bfloat16 [4096, 65536], P(None, ('grp', 'fsdp')), may hold values from -0.09375 to 0.09375
- targets: int32 [4096], P(('grp', 'fsdp')), may hold values from 0 to 65535
- ranks: int32 [4096], P(('grp', 'fsdp')), may hold values from 0 to 2047, as said below
- train_input: bfloat16 [4096, 8192], P(('grp', 'fsdp')), may hold values from -6 to 6
- cotangent: bfloat16 [4096, 8192], P(('grp', 'fsdp')), may hold values from -6 to 6
- w_gate: bfloat16 [14336, 8192], P('fsdp', 'grp'), may hold values from -0.0625 to 0.0625
- w_up: bfloat16 [14336, 8192], P('fsdp', 'grp'), may hold values from -0.0625 to 0.0625
- w_down: bfloat16 [14336, 8192], P('fsdp', 'grp'), may hold values from -0.046875 to 0.046875
Outputs:
- token_loss: float32 [4096], P(('grp', 'fsdp'))
- grad_gate: bfloat16 [14336, 8192], P('fsdp', 'grp')
- grad_up: bfloat16 [14336, 8192], P('fsdp', 'grp')
- grad_down: bfloat16 [14336, 8192], P('fsdp', 'grp')
The draws below stay inside these ranges and needn't reach their ends.
Inputs may be any that keep to these rules, and one draw needn't show every extreme that they name: Within each half of the tokens (the first 2048 and the last 2048) the ranks are a permutation of 0 to 2047. The 128 tokens of one device hold at most 2 with rank under 16, and some device holds exactly 2.
All inputs are finite; a program needn't handle non-finite values.
Results may differ from the reference program's by a relative error of at most 0.005.
Values may be sent and summed in bfloat16 or wider, within the bound.
A program may use at most 384 MiB of HBM per device.

```python
import jax
import jax.numpy as jnp
from jax import lax

D = 8192
FW = 14336
DS = 4096
VS = 65536
TOK_DEV = 128
CAP = 2
HALF = 2048
TOKENS = 4096
KEEP_HALF = 16
KEEP_TOTAL = 32
N_FSDP = 16


def draw_scorer_gain(key, part):
    key = jax.random.fold_in(key, 5)
    return 1.0 + 0.1 * jax.random.normal(key, (DS,), jnp.float32)


def draw_ranks(key, part):
    key = jax.random.fold_in(key, 11)
    key_load, key_shuffle, key_place, key_score = jax.random.split(key, 4)
    pair_load = jax.random.randint(key_load, (2, N_FSDP // 2), 0, CAP + 1)
    pair_load = pair_load.at[:, 0].set(CAP)
    device_load = jnp.concatenate([pair_load, CAP - pair_load], axis=1)
    shuffle_score = jax.random.randint(key_shuffle, (2, N_FSDP), 0, 2 ** 20) * N_FSDP + jnp.arange(N_FSDP, dtype=jnp.int32)[None, :]
    device_order = jnp.argsort(shuffle_score, axis=1)
    device_load = jnp.take_along_axis(device_load, device_order, axis=1)
    place_score = jax.random.randint(key_place, (2, N_FSDP, TOK_DEV), 0, 2 ** 20) * TOK_DEV + jnp.arange(TOK_DEV, dtype=jnp.int32)[None, None, :]
    slot_place = jnp.argsort(jnp.argsort(place_score, axis=2), axis=2)
    chosen = slot_place < device_load[:, :, None]
    base_score = jax.random.randint(key_score, (2, HALF), 0, 2 ** 8)
    level = jnp.where(chosen.reshape(2, HALF), 0, 2 ** 8)
    full_score = (level + base_score) * HALF + jnp.arange(HALF, dtype=jnp.int32)[None, :]
    ranking = jnp.argsort(jnp.argsort(full_score, axis=1), axis=1)
    return ranking.reshape(TOKENS).astype(jnp.int32)


def plant(entries, rng, low, largest):
    shape = entries.shape
    place = [jax.random.randint(jax.random.fold_in(rng, axis), (), 0, shape[axis]) for axis in range(len(shape))]
    entries = entries.at[tuple(place)].set(low)
    longest = shape.index(max(shape))
    place[longest] = (place[longest] + 1) % shape[longest]
    return entries.at[tuple(place)].set(largest)


def level_of(own_key, dims, cuts, least, largest):
    def one(axis_at, shards_of):
        heights = jax.random.uniform(jax.random.fold_in(jax.random.fold_in(own_key, 6), axis_at), (shards_of,), jnp.float32, least / len(cuts), largest / len(cuts))
        return jnp.repeat(jnp.exp(heights), dims[axis_at] // shards_of).reshape((-1,) + (1,) * (len(dims) - axis_at - 1))

    gain = one(*cuts[0])
    for cut in cuts[1:]:
        gain = gain * one(*cut)
    return gain


def normal_values(stream_key, dims, deviation, limit, cuts=(), kind=jnp.bfloat16):
    drawn = deviation * jax.random.normal(stream_key, dims, jnp.float32)
    if cuts:
        drawn = drawn * level_of(stream_key, dims, cuts, -0.22, 0.18)
    return jnp.clip(drawn, -limit, limit).astype(kind)


def setup_inputs(seed: int = 0) -> dict:
    seeds = jax.random.split(jax.random.key(seed), 11)
    return {
        "scorer_hidden": normal_values(seeds[0], (TOKENS, DS), 1.0, 6.0, ((0, 32),)),
        "scorer_gain": draw_scorer_gain(jax.random.fold_in(seeds[10], 71), 0),
        "scorer_head": normal_values(seeds[2], (DS, VS), DS ** -0.5, 0.09375, ((1, 32),)),
        "targets": plant(jax.random.randint(seeds[3], (TOKENS,), 0, VS), jax.random.fold_in(seeds[3], 1), 0, VS - 1).astype(jnp.int32),
        "ranks": draw_ranks(jax.random.fold_in(seeds[10], 71), 0),
        "train_input": normal_values(seeds[5], (TOKENS, D), 1.0, 6.0, ((0, 32),)),
        "cotangent": normal_values(seeds[6], (TOKENS, D), 1.0, 6.0, ((0, 32),)),
        "w_gate": normal_values(seeds[7], (FW, D), D ** -0.5, 0.0625, ((0, 16), (1, 2))),
        "w_up": normal_values(seeds[8], (FW, D), D ** -0.5, 0.0625, ((0, 16), (1, 2))),
        "w_down": normal_values(seeds[9], (FW, D), FW ** -0.5, 0.046875, ((0, 16), (1, 2))),
    }


def score_block(normed_block, target_block, scorer_head):
    logits = jnp.dot(normed_block, scorer_head, preferred_element_type=jnp.float32)
    highest = lax.optimization_barrier(jnp.max(logits, axis=1))
    log_total = highest + jnp.log(lax.optimization_barrier(jnp.sum(jnp.exp(logits - highest[:, None]), axis=1)))
    target_logit = jnp.take_along_axis(logits, target_block[:, None].astype(jnp.int32), axis=1)[:, 0]
    return log_total - target_logit

def reference(scorer_hidden, scorer_gain, scorer_head, targets, ranks, train_input, cotangent, w_gate, w_up, w_down):
    by_half = jnp.argsort(ranks.reshape(2, HALF), axis=1)[:, :KEEP_HALF].astype(jnp.int32)
    offsets = (jnp.arange(2, dtype=jnp.int32) * HALF)[:, None]
    chosen_index = (by_half + offsets).reshape(KEEP_TOTAL).astype(jnp.int32)
    hidden_rows = scorer_hidden[chosen_index].astype(jnp.float32)
    mean_square = lax.optimization_barrier(jnp.mean(hidden_rows * hidden_rows, axis=1, keepdims=True))
    normed = (hidden_rows * lax.rsqrt(mean_square + 1e-05) * scorer_gain.astype(jnp.float32)).astype(jnp.bfloat16)
    target_rows = targets[chosen_index]
    block_rows = 32
    losses = lax.map(lambda pair: score_block(pair[0], pair[1], scorer_head), (normed.reshape(KEEP_TOTAL // block_rows, block_rows, DS), target_rows.reshape(KEEP_TOTAL // block_rows, block_rows)))
    losses = losses.reshape(KEEP_TOTAL)
    token_loss = jnp.zeros((TOKENS,), jnp.float32).at[chosen_index].set(losses)
    inputs = train_input[chosen_index]
    upstream = cotangent[chosen_index]
    gate = jnp.dot(inputs, w_gate.T, preferred_element_type=jnp.float32)
    up_part = jnp.dot(inputs, w_up.T, preferred_element_type=jnp.float32)
    sigmoid_gate = jax.nn.sigmoid(gate)
    act = gate * sigmoid_gate
    hidden = (act * up_part).astype(jnp.bfloat16)
    grad_down = jnp.dot(hidden.T, upstream, preferred_element_type=jnp.float32).astype(jnp.bfloat16)
    dhidden = jnp.dot(upstream, w_down.T, preferred_element_type=jnp.float32)
    dgate = (dhidden * up_part * sigmoid_gate * (1.0 + gate * (1.0 - sigmoid_gate))).astype(jnp.bfloat16)
    dup = (dhidden * act).astype(jnp.bfloat16)
    grad_gate = jnp.dot(dgate.T, inputs, preferred_element_type=jnp.float32).astype(jnp.bfloat16)
    grad_up = jnp.dot(dup.T, inputs, preferred_element_type=jnp.float32).astype(jnp.bfloat16)
    return (token_loss, grad_gate, grad_up, grad_down)
```

```python
import jax
import jax.numpy as jnp
from jax import lax
from jax.sharding import PartitionSpec as P

CAP = 2


def on_device(
    scorer_hidden,
    scorer_gain,
    scorer_head,
    targets,
    ranks,
    train_input,
    cotangent,
    w_gate,
    w_up,
    w_down,
):
    slot_count = CAP
    shard_count = lax.axis_size("fsdp")
    keep_half = shard_count * slot_count // 2
    own_index = lax.axis_index("grp") * shard_count + lax.axis_index("fsdp")
    chosen = (ranks < keep_half).astype(jnp.int32)
    slot_place = jnp.cumsum(chosen) - 1
    slot_ids = lax.iota(jnp.int32, slot_count)
    picker = (slot_place[None, :] == slot_ids[:, None]) & (chosen[None, :] > 0)
    pick_bf = picker.astype(jnp.bfloat16)
    hidden_rows = jnp.dot(pick_bf, scorer_hidden, preferred_element_type=jnp.float32)
    target_rows = jnp.sum(picker.astype(jnp.int32) * targets[None, :], axis=1)
    mean_square = jnp.mean(hidden_rows * hidden_rows, axis=1, keepdims=True)
    normed = (hidden_rows * lax.rsqrt(mean_square + 1e-05) * scorer_gain[None, :]).astype(
        jnp.bfloat16
    )
    input_rows = jnp.dot(pick_bf, train_input, preferred_element_type=jnp.float32).astype(
        jnp.bfloat16
    )
    cotangent_rows = jnp.dot(pick_bf, cotangent, preferred_element_type=jnp.float32).astype(
        jnp.bfloat16
    )
    score_width = scorer_hidden.shape[1]
    model_width = train_input.shape[1]
    half_width = w_gate.shape[1]
    packed = jnp.concatenate([normed, input_rows, cotangent_rows], axis=1)
    gathered, target_all = (
        lax.all_gather(packed, ("grp", "fsdp"), axis=0, tiled=True),
        lax.all_gather(target_rows, ("grp", "fsdp"), axis=0, tiled=True),
    )
    normed_all = gathered[:, :score_width]
    column = lax.axis_index("grp") * half_width
    inputs = lax.dynamic_slice_in_dim(gathered, score_width + column, half_width, axis=1)
    upstream = lax.dynamic_slice_in_dim(
        gathered, score_width + model_width + column, half_width, axis=1
    )

    def part(rows, weights):
        return jnp.einsum("sd,fd->sf", rows, weights, preferred_element_type=jnp.float32)

    parts = jnp.concatenate(
        [part(inputs, w_gate), part(inputs, w_up), part(upstream, w_down)], axis=1
    )
    gate, up_part, dhidden = jnp.split(lax.psum(parts, "grp"), 3, axis=1)
    logits = jnp.dot(normed_all, scorer_head, preferred_element_type=jnp.float32)
    vocab_width = scorer_head.shape[1]
    vocab_start = own_index * vocab_width
    target_hit = target_all[:, None] - vocab_start == lax.iota(jnp.int32, vocab_width)[None, :]
    highest = jnp.max(logits, axis=1)
    target_logit = jnp.sum(jnp.where(target_hit, logits, 0.0), axis=1)
    rescaled = jnp.sum(jnp.exp(logits - highest[:, None]), axis=1)
    stats = lax.all_gather(jnp.stack([highest, rescaled, target_logit]), ("grp", "fsdp"), axis=0)
    own = lax.dynamic_slice_in_dim(stats, own_index * slot_count, slot_count, axis=2)
    peak = jnp.max(own[:, 0], axis=0)
    total = jnp.sum(own[:, 1] * jnp.exp(own[:, 0] - peak[None, :]), axis=0)
    own_losses = peak + jnp.log(total) - jnp.sum(own[:, 2], axis=0)
    token_loss = jnp.sum(picker.astype(jnp.float32) * own_losses[:, None], axis=0)
    sigmoid_gate = jax.nn.sigmoid(gate)
    act = gate * sigmoid_gate
    hidden = (act * up_part).astype(jnp.bfloat16)
    dgate = (dhidden * up_part * sigmoid_gate * (1.0 + gate * (1.0 - sigmoid_gate))).astype(
        jnp.bfloat16
    )
    dup = (dhidden * act).astype(jnp.bfloat16)

    def outer(left, right):
        return jnp.einsum("sf,sd->fd", left, right, preferred_element_type=jnp.float32).astype(
            jnp.bfloat16
        )

    return token_loss, outer(dgate, inputs), outer(dup, inputs), outer(hidden, upstream)


def solution(mesh):
    in_specs = (
        P(("grp", "fsdp"), None),
        P(),
        P(None, ("grp", "fsdp")),
        P(("grp", "fsdp")),
        P(("grp", "fsdp")),
        P(("grp", "fsdp"), None),
        P(("grp", "fsdp"), None),
        P("fsdp", "grp"),
        P("fsdp", "grp"),
        P("fsdp", "grp"),
    )
    out_specs = (P(("grp", "fsdp")), P("fsdp", "grp"), P("fsdp", "grp"), P("fsdp", "grp"))
    return jax.shard_map(
        on_device, mesh=mesh, in_specs=in_specs, out_specs=out_specs, check_vma=False
    )
```

```python
import functools

import jax
import jax.numpy as jnp
from jax import lax
from jax.experimental import pallas as pl
from jax.experimental.pallas import tpu as pltpu
from jax.sharding import PartitionSpec as P

CAP = 2
SLOTS = 2 * CAP
QUARTERS = 4
ROWS = SLOTS * QUARTERS
F32 = jnp.float32
BF16 = jnp.bfloat16
MESH = pl.DeviceIdType.MESH


def exchange_kernel(
    n,
    gain_ref,
    targets_ref,
    ranks_ref,
    hidden_hbm,
    input_hbm,
    cot_hbm,
    gate_hbm,
    up_hbm,
    down_hbm,
    head_hbm,
    loss_ref,
    left_ref,
    x_ref,
    u_ref,
    hidden_v,
    input_v,
    cot_v,
    weight_v,
    head_v,
    block_v,
    mate_v,
    gather_v,
    normed_v,
    part_v,
    other_v,
    logits_v,
    stat_v,
    stat_in,
    load_sem,
    send_sem,
    mate_sem,
    gather_sem,
    normed_sem,
    part_sem,
    stat_sem,
):
    groups = n // 4
    slots = n * SLOTS
    core = lax.axis_index("grp")
    chip = lax.axis_index("fsdp")
    a, b, c = chip // 4, lax.rem(chip // 2, 2), lax.rem(chip, 2)

    def at(a_, b_, c_):
        return a_ * 4 + b_ * 2 + c_

    mate = (1 - core, chip)
    y_peer = (core, at(a, 1 - b, c))
    x_peer = (core, at(a, b, 1 - c))
    z_to = [(core, at(lax.rem(a + d, groups), b, c)) for d in range(1, groups)]
    peers = [mate, y_peer, x_peer] + z_to

    loads = [
        pltpu.make_async_copy(src, dst, load_sem.at[i])
        for i, (src, dst) in enumerate(
            [
                (hidden_hbm, hidden_v),
                (input_hbm, input_v),
                (cot_hbm, cot_v),
                (gate_hbm, weight_v.at[0]),
                (up_hbm, weight_v.at[1]),
                (down_hbm, weight_v.at[2]),
                (head_hbm, head_v),
            ]
        )
    ]
    for load in loads:
        load.start()

    barrier = pltpu.get_barrier_semaphore()
    for peer in peers:
        pl.semaphore_signal(barrier, inc=1, device_id=peer, device_id_type=MESH)

    sends = []

    def send(src, dst, recv_sem, peer):
        copy = pltpu.make_async_remote_copy(
            src_ref=src,
            dst_ref=dst,
            send_sem=send_sem.at[len(sends)],
            recv_sem=recv_sem,
            device_id=peer,
            device_id_type=MESH,
        )
        copy.start()
        sends.append(copy)

    def arrived(dst, recv_sem, peer):
        pltpu.make_async_remote_copy(
            src_ref=dst,
            dst_ref=dst,
            send_sem=send_sem.at[0],
            recv_sem=recv_sem,
            device_id=peer,
            device_id_type=MESH,
        ).wait_recv()

    tokens = ranks_ref.shape[1]
    half = weight_v.shape[2]
    piece = half // QUARTERS
    score = hidden_v.shape[1]
    score_half = score // 2
    score_piece = score_half // QUARTERS
    keep_half = n * CAP // 2
    chosen = ranks_ref[...] < keep_half
    chosen_rows = jnp.broadcast_to(chosen.astype(F32), (16, tokens)).astype(BF16)
    before = (
        lax.broadcasted_iota(jnp.int32, (tokens, tokens), 0)
        < lax.broadcasted_iota(jnp.int32, (tokens, tokens), 1)
    ).astype(F32).astype(BF16)
    place = jnp.dot(chosen_rows, before, preferred_element_type=F32).astype(jnp.int32)
    row = lax.broadcasted_iota(jnp.int32, (ROWS, tokens), 0)
    row_slot = lax.rem(row, SLOTS) - core * CAP
    picked = (place == row_slot) & (chosen_rows.astype(F32) > 0)
    picks = [
        (picked & (row // SLOTS == q)).astype(F32).astype(BF16) for q in range(QUARTERS)
    ]

    def select(ref, start, width):
        total = None
        for q in range(QUARTERS):
            term = jnp.dot(
                picks[q],
                ref[:, start + q * width : start + (q + 1) * width],
                preferred_element_type=F32,
            )
            total = term if total is None else total + term
        return total

    targets = targets_ref[...]
    first = (picked & (row < SLOTS)).astype(F32)
    high = jnp.sum(first * (targets // 256).astype(F32), axis=1, keepdims=True)
    low = jnp.sum(first * lax.rem(targets, 256).astype(F32), axis=1, keepdims=True)
    lane = lax.broadcasted_iota(jnp.int32, (ROWS, 128), 1)
    digits = jnp.where(lane == 0, high, jnp.where(lane == 1, low, 0.0)).astype(BF16)

    loads[0].wait()
    halves = [select(hidden_v, h * score_half, score_piece) for h in range(2)]
    square = sum(jnp.sum(v * v, axis=1, keepdims=True) for v in halves)
    square = sum(square[q * SLOTS : (q + 1) * SLOTS] for q in range(QUARTERS))
    scale = lax.rsqrt(square / score + 1e-05)
    scale = jnp.concatenate([scale] * QUARTERS, axis=0)
    piece_row = lax.broadcasted_iota(jnp.int32, (ROWS, score_piece), 0) // SLOTS
    tail = 2 * piece
    end = tail + score_piece
    for h in range(2):
        gain = jnp.zeros((ROWS, score_piece), F32)
        for q in range(QUARTERS):
            start = h * score_half + q * score_piece
            gain = jnp.where(piece_row == q, gain_ref[:, start : start + score_piece], gain)
        block_v[h, :, tail:end] = (halves[h] * scale * gain).astype(BF16)
        block_v[h, :, end:] = digits
    loads[1].wait()
    loads[2].wait()
    for h in range(2):
        block_v[h, :, :piece] = select(input_v, h * half, piece).astype(BF16)
        block_v[h, :, piece:tail] = select(cot_v, h * half, piece).astype(BF16)

    pl.semaphore_wait(barrier, len(peers))
    send(block_v.at[1 - core], mate_v, mate_sem.at[0], mate)
    arrived(mate_v, mate_sem.at[0], mate)
    gather_v[chip] = block_v[core] + mate_v[...]

    width = gather_v.shape[2]
    cut = (width // 128 + 1) // 2 * 128
    z_sem, y_sem, x_sem, ya_sem, xb_sem = (gather_sem.at[i] for i in range(5))
    for d in range(1, groups):
        own = gather_v.at[chip]
        send(own, own, z_sem.at[d], z_to[d - 1])
    for d in range(groups):
        source = lax.rem(a + groups - d, groups)
        block = gather_v.at[at(source, b, c)]
        if d:
            arrived(block, z_sem.at[d], (core, at(source, b, c)))
        send(block, block, y_sem.at[d], y_peer)
        send(block, block, x_sem.at[d], x_peer)
    for d in range(groups):
        source = lax.rem(a + groups - d, groups)
        block = gather_v.at[at(source, 1 - b, c)]
        arrived(block, y_sem.at[d], y_peer)
        block = block.at[:, pl.ds(0, cut)]
        send(block, block, xb_sem.at[d], x_peer)
        block = gather_v.at[at(source, b, 1 - c)]
        arrived(block, x_sem.at[d], x_peer)
        block = block.at[:, pl.ds(cut, width - cut)]
        send(block, block, ya_sem.at[d], y_peer)
    for d in range(groups):
        source = lax.rem(a + groups - d, groups)
        block = gather_v.at[at(source, 1 - b, 1 - c)]
        arrived(block.at[:, pl.ds(0, cut)], xb_sem.at[d], x_peer)
        arrived(block.at[:, pl.ds(cut, width - cut)], ya_sem.at[d], y_peer)

    def take(q, start, stop):
        rows = gather_v[:, :, start:stop].reshape(n * ROWS, stop - start)
        slot = lax.broadcasted_iota(jnp.int32, (slots, n * ROWS), 0)
        place = lax.broadcasted_iota(jnp.int32, (slots, n * ROWS), 1)
        wanted = slot // SLOTS * ROWS + q * SLOTS + lax.rem(slot, SLOTS)
        pick = (place == wanted).astype(F32).astype(BF16)
        return jnp.dot(pick, rows, preferred_element_type=F32)

    for q in range(QUARTERS):
        normed_v[core, :, q * score_piece : (q + 1) * score_piece] = take(q, tail, end).astype(
            BF16
        )
    send(normed_v.at[core], normed_v.at[core], normed_sem.at[0], mate)
    digits = take(0, end, width)
    target = (digits[:, 0:1] * 256.0 + digits[:, 1:2]).astype(jnp.int32)
    for q in range(QUARTERS):
        x_ref[:, q * piece : (q + 1) * piece] = take(q, 0, piece).astype(BF16)
        u_ref[:, q * piece : (q + 1) * piece] = take(q, piece, tail).astype(BF16)

    units = weight_v.shape[1]
    tile = units // 2 if units % 256 == 0 else units
    for i, rows in enumerate([x_ref, x_ref, u_ref]):
        loads[3 + i].wait()

        @pl.loop(0, units // tile)
        def _(j):
            at_units = pl.ds(pl.multiple_of(j * tile, tile), tile)
            part_v[i, at_units, :] = lax.dot_general(
                weight_v[i, at_units, :],
                rows[...],
                (((1,), (1,)), ((), ())),
                preferred_element_type=F32,
            )

        send(part_v.at[i], other_v.at[i], part_sem.at[i], mate)

    loads[6].wait()
    arrived(normed_v.at[1 - core], normed_sem.at[0], mate)
    vocab = head_v.shape[1]
    v_tile = 256

    @pl.loop(0, vocab // v_tile)
    def _(j):
        at_vocab = pl.ds(pl.multiple_of(j * v_tile, v_tile), v_tile)
        logits_v[:, at_vocab] = jnp.dot(
            normed_v[0], head_v[:score_half, at_vocab], preferred_element_type=F32
        ) + jnp.dot(normed_v[1], head_v[score_half:, at_vocab], preferred_element_type=F32)

    logits = logits_v[...]
    entry = lax.broadcasted_iota(jnp.int32, (slots, vocab), 1)
    hit = entry == target - (core * n + chip) * vocab
    peak = jnp.max(logits, axis=1, keepdims=True)
    total = jnp.sum(jnp.exp(logits - peak), axis=1, keepdims=True)
    wanted = jnp.sum(jnp.where(hit, logits, 0.0), axis=1, keepdims=True)
    lane = lax.broadcasted_iota(jnp.int32, (slots, 128), 1)

    def pack(stats):
        return jnp.where(lane == 0, stats[0], jnp.where(lane == 1, stats[1], stats[2]))

    def combine(terms):
        peak = functools.reduce(jnp.maximum, [t[0] for t in terms])
        total = sum(t[1] * jnp.exp(t[0] - peak) for t in terms)
        return peak, total, sum(t[2] for t in terms)

    def split(packed):
        return packed[:, 0:1], packed[:, 1:2], packed[:, 2:3]

    stats = (peak, total, wanted)

    def multiply(i):
        arrived(other_v.at[i], part_sem.at[i], mate)
        return part_v[i] + other_v[i]

    for i, peer in enumerate([mate, x_peer, y_peer]):
        stat_v[i] = pack(stats)
        send(stat_v.at[i], stat_in.at[i], stat_sem.at[i], peer)
        if i == 0:
            gate = multiply(0)
            up = multiply(1)
            s = jax.nn.sigmoid(gate)
            act = gate * s
            left_ref[2] = (act * up).astype(BF16)
            dhidden = multiply(2)
            left_ref[0] = (dhidden * up * s * (1.0 + gate * (1.0 - s))).astype(BF16)
            left_ref[1] = (dhidden * act).astype(BF16)
        arrived(stat_in.at[i], stat_sem.at[i], peer)
        stats = combine([stats, split(stat_in[i])])
    stat_v[3] = pack(stats)
    for d in range(1, groups):
        send(stat_v.at[3], stat_in.at[2 + d], stat_sem.at[2 + d], z_to[d - 1])
    terms = [stats]
    for d in range(1, groups):
        source = (core, at(lax.rem(a + groups - d, groups), b, c))
        arrived(stat_in.at[2 + d], stat_sem.at[2 + d], source)
        terms.append(split(stat_in[2 + d]))
    peak, total, wanted = combine(terms)
    losses = peak + jnp.log(total) - wanted
    slot = lax.broadcasted_iota(jnp.int32, (slots, tokens), 0)
    mine = slot == place[0:1] + chip * SLOTS + core * CAP
    mine = mine & (jnp.broadcast_to(ranks_ref[...], (slots, tokens)) < keep_half)
    loss_ref[...] = jnp.sum(jnp.where(mine, losses, 0.0), axis=0, keepdims=True)
    for copy in sends:
        copy.wait_send()


def outer_kernel(left_ref, x_ref, u_ref, gate_ref, up_ref, down_ref):
    for i, (right, out) in enumerate([(x_ref, gate_ref), (x_ref, up_ref), (u_ref, down_ref)]):
        width = out.shape[1]
        step = 1024 if width % 1024 == 0 else width
        for k in range(width // step):
            out[:, k * step : (k + 1) * step] = jnp.dot(
                left_ref[i], right[:, k * step : (k + 1) * step], preferred_element_type=F32
            ).astype(BF16)


def on_device(
    scorer_hidden,
    scorer_gain,
    scorer_head,
    targets,
    ranks,
    train_input,
    cotangent,
    w_gate,
    w_up,
    w_down,
):
    n = lax.axis_size("fsdp")
    groups = n // 4
    slots = n * SLOTS
    score, vocab = scorer_head.shape
    units, half = w_gate.shape
    tokens = ranks.shape[0]
    width = 2 * half // QUARTERS + score // 2 // QUARTERS + 128
    vmem = pl.BlockSpec(memory_space=pltpu.VMEM)
    hbm = pl.BlockSpec(memory_space=pl.ANY)
    n_sends = 1 + (groups - 1) + 4 * groups + 1 + 3 + 3 + (groups - 1)
    dma = pltpu.SemaphoreType.DMA
    loss, left, inputs, upstream = pl.pallas_call(
        functools.partial(exchange_kernel, n),
        out_shape=(
            jax.ShapeDtypeStruct((1, tokens), F32),
            jax.ShapeDtypeStruct((3, units, slots), BF16),
            jax.ShapeDtypeStruct((slots, half), BF16),
            jax.ShapeDtypeStruct((slots, half), BF16),
        ),
        in_specs=[vmem] * 3 + [hbm] * 7,
        out_specs=(vmem,) * 4,
        scratch_shapes=[
            pltpu.VMEM(scorer_hidden.shape, BF16),
            pltpu.VMEM(train_input.shape, BF16),
            pltpu.VMEM(cotangent.shape, BF16),
            pltpu.VMEM((3, units, half), BF16),
            pltpu.VMEM((score, vocab), BF16),
            pltpu.VMEM((2, ROWS, width), BF16),
            pltpu.VMEM((ROWS, width), BF16),
            pltpu.VMEM((n, ROWS, width), BF16),
            pltpu.VMEM((2, slots, score // 2), BF16),
            pltpu.VMEM((3, units, slots), F32),
            pltpu.VMEM((3, units, slots), F32),
            pltpu.VMEM((slots, vocab), F32),
            pltpu.VMEM((4, slots, 128), F32),
            pltpu.VMEM((2 + groups, slots, 128), F32),
            dma((7,)),
            dma((n_sends,)),
            dma((1,)),
            dma((5, groups)),
            dma((1,)),
            dma((3,)),
            dma((2 + groups,)),
        ],
        compiler_params=pltpu.CompilerParams(
            collective_id=0, has_side_effects=True, vmem_limit_bytes=60 * 2**20
        ),
    )(
        scorer_gain.reshape(1, score),
        targets.reshape(1, tokens),
        ranks.reshape(1, tokens),
        scorer_hidden,
        train_input,
        cotangent,
        w_gate,
        w_up,
        w_down,
        scorer_head,
    )
    tile = 128 if units % 128 == 0 else units
    whole = pl.BlockSpec((slots, half), lambda i: (0, 0))
    out = pl.BlockSpec((tile, half), lambda i: (i, 0))
    grads = pl.pallas_call(
        outer_kernel,
        grid=(units // tile,),
        out_shape=(jax.ShapeDtypeStruct((units, half), BF16),) * 3,
        in_specs=[pl.BlockSpec((3, tile, slots), lambda i: (0, i, 0)), whole, whole],
        out_specs=(out,) * 3,
        compiler_params=pltpu.CompilerParams(vmem_limit_bytes=48 * 2**20),
    )(left, inputs, upstream)
    return (loss.reshape(tokens),) + tuple(grads)


def solution(mesh):
    in_specs = (
        P(("grp", "fsdp"), None),
        P(),
        P(None, ("grp", "fsdp")),
        P(("grp", "fsdp")),
        P(("grp", "fsdp")),
        P(("grp", "fsdp"), None),
        P(("grp", "fsdp"), None),
        P("fsdp", "grp"),
        P("fsdp", "grp"),
        P("fsdp", "grp"),
    )
    out_specs = (P(("grp", "fsdp")), P("fsdp", "grp"), P("fsdp", "grp"), P("fsdp", "grp"))
    return jax.shard_map(
        on_device, mesh=mesh, in_specs=in_specs, out_specs=out_specs, check_vma=False
    )
```

```python
import functools

import jax
import jax.numpy as jnp
from jax import lax
from jax.experimental import pallas as pl
from jax.experimental.pallas import tpu as pltpu
from jax.sharding import PartitionSpec as P

CAP = 2
SLOTS = 2 * CAP
QUARTERS = 4
ROWS = SLOTS * QUARTERS
F32 = jnp.float32
BF16 = jnp.bfloat16
MESH = pl.DeviceIdType.MESH


def exchange_kernel(
    n,
    gain_ref,
    targets_ref,
    ranks_ref,
    hidden_hbm,
    input_hbm,
    cot_hbm,
    gate_hbm,
    up_hbm,
    down_hbm,
    head_hbm,
    loss_ref,
    left_ref,
    x_ref,
    u_ref,
    hidden_v,
    input_v,
    cot_v,
    weight_v,
    head_v,
    block_v,
    mate_v,
    gather_v,
    normed_v,
    part_v,
    other_v,
    logits_v,
    stat_v,
    stat_in,
    load_sem,
    send_sem,
    mate_sem,
    gather_sem,
    normed_sem,
    part_sem,
    stat_sem,
):
    groups = n // 4
    slots = n * SLOTS
    core = lax.axis_index("grp")
    chip = lax.axis_index("fsdp")
    a, b, c = chip // 4, lax.rem(chip // 2, 2), lax.rem(chip, 2)

    def at(a_, b_, c_):
        return a_ * 4 + b_ * 2 + c_

    mate = (1 - core, chip)
    y_peer = (core, at(a, 1 - b, c))
    x_peer = (core, at(a, b, 1 - c))
    z_to = [(core, at(lax.rem(a + d, groups), b, c)) for d in range(1, groups)]
    peers = [mate, y_peer, x_peer] + z_to

    loads = [
        pltpu.make_async_copy(src, dst, load_sem.at[i])
        for i, (src, dst) in enumerate(
            [
                (hidden_hbm, hidden_v),
                (input_hbm, input_v),
                (cot_hbm, cot_v),
                (gate_hbm, weight_v.at[0]),
                (up_hbm, weight_v.at[1]),
                (down_hbm, weight_v.at[2]),
                (head_hbm, head_v),
            ]
        )
    ]
    for load in loads[:3]:
        load.start()

    barrier = pltpu.get_barrier_semaphore()
    for peer in peers:
        pl.semaphore_signal(barrier, inc=1, device_id=peer, device_id_type=MESH)

    sends = []

    def send(src, dst, recv_sem, peer):
        copy = pltpu.make_async_remote_copy(
            src_ref=src,
            dst_ref=dst,
            send_sem=send_sem.at[len(sends)],
            recv_sem=recv_sem,
            device_id=peer,
            device_id_type=MESH,
        )
        copy.start()
        sends.append(copy)

    def arrived(dst, recv_sem, peer):
        pltpu.make_async_remote_copy(
            src_ref=dst,
            dst_ref=dst,
            send_sem=send_sem.at[0],
            recv_sem=recv_sem,
            device_id=peer,
            device_id_type=MESH,
        ).wait_recv()

    tokens = ranks_ref.shape[1]
    half = weight_v.shape[2]
    piece = half // QUARTERS
    score = hidden_v.shape[1]
    score_half = score // 2
    score_piece = score_half // QUARTERS
    keep_half = n * CAP // 2
    chosen = ranks_ref[...] < keep_half
    chosen_rows = jnp.broadcast_to(chosen.astype(F32), (16, tokens)).astype(BF16)
    before = (
        lax.broadcasted_iota(jnp.int32, (tokens, tokens), 0)
        < lax.broadcasted_iota(jnp.int32, (tokens, tokens), 1)
    ).astype(F32).astype(BF16)
    place = jnp.dot(chosen_rows, before, preferred_element_type=F32).astype(jnp.int32)
    row = lax.broadcasted_iota(jnp.int32, (ROWS, tokens), 0)
    row_slot = lax.rem(row, SLOTS) - core * CAP
    picked = (place == row_slot) & (chosen_rows.astype(F32) > 0)
    picks = [
        (picked & (row // SLOTS == q)).astype(F32).astype(BF16) for q in range(QUARTERS)
    ]

    def select(ref, start, width):
        total = None
        for q in range(QUARTERS):
            term = jnp.dot(
                picks[q],
                ref[:, start + q * width : start + (q + 1) * width],
                preferred_element_type=F32,
            )
            total = term if total is None else total + term
        return total

    targets = targets_ref[...]
    first = (picked & (row < SLOTS)).astype(F32)
    high = jnp.sum(first * (targets // 256).astype(F32), axis=1, keepdims=True)
    low = jnp.sum(first * lax.rem(targets, 256).astype(F32), axis=1, keepdims=True)
    lane = lax.broadcasted_iota(jnp.int32, (ROWS, 128), 1)
    digits = jnp.where(lane == 0, high, jnp.where(lane == 1, low, 0.0)).astype(BF16)

    for load in loads[:3]:
        load.wait()
    for load in loads[3:]:
        load.start()
    halves = [select(hidden_v, h * score_half, score_piece) for h in range(2)]
    square = sum(jnp.sum(v * v, axis=1, keepdims=True) for v in halves)
    square = sum(square[q * SLOTS : (q + 1) * SLOTS] for q in range(QUARTERS))
    scale = lax.rsqrt(square / score + 1e-05)
    scale = jnp.concatenate([scale] * QUARTERS, axis=0)
    piece_row = lax.broadcasted_iota(jnp.int32, (ROWS, score_piece), 0) // SLOTS
    tail = 2 * piece
    end = tail + score_piece
    for h in range(2):
        gain = jnp.zeros((ROWS, score_piece), F32)
        for q in range(QUARTERS):
            start = h * score_half + q * score_piece
            gain = jnp.where(piece_row == q, gain_ref[:, start : start + score_piece], gain)
        block_v[h, :, tail:end] = (halves[h] * scale * gain).astype(BF16)
        block_v[h, :, end:] = digits
    for h in range(2):
        block_v[h, :, :piece] = select(input_v, h * half, piece).astype(BF16)
        block_v[h, :, piece:tail] = select(cot_v, h * half, piece).astype(BF16)

    pl.semaphore_wait(barrier, len(peers))
    send(block_v.at[1 - core], mate_v, mate_sem.at[0], mate)
    arrived(mate_v, mate_sem.at[0], mate)
    gather_v[chip] = block_v[core] + mate_v[...]

    width = gather_v.shape[2]
    cut = (width // 128 + 1) // 2 * 128
    z_sem, y_sem, x_sem, ya_sem, xb_sem = (gather_sem.at[i] for i in range(5))
    for d in range(1, groups):
        own = gather_v.at[chip]
        send(own, own, z_sem.at[d], z_to[d - 1])
    for d in range(groups):
        source = lax.rem(a + groups - d, groups)
        block = gather_v.at[at(source, b, c)]
        if d:
            arrived(block, z_sem.at[d], (core, at(source, b, c)))
        send(block, block, y_sem.at[d], y_peer)
        send(block, block, x_sem.at[d], x_peer)
    for d in range(groups):
        source = lax.rem(a + groups - d, groups)
        block = gather_v.at[at(source, 1 - b, c)]
        arrived(block, y_sem.at[d], y_peer)
        block = block.at[:, pl.ds(0, cut)]
        send(block, block, xb_sem.at[d], x_peer)
        block = gather_v.at[at(source, b, 1 - c)]
        arrived(block, x_sem.at[d], x_peer)
        block = block.at[:, pl.ds(cut, width - cut)]
        send(block, block, ya_sem.at[d], y_peer)
    for d in range(groups):
        source = lax.rem(a + groups - d, groups)
        block = gather_v.at[at(source, 1 - b, 1 - c)]
        arrived(block.at[:, pl.ds(0, cut)], xb_sem.at[d], x_peer)
        arrived(block.at[:, pl.ds(cut, width - cut)], ya_sem.at[d], y_peer)

    def take(q, start, stop):
        rows = gather_v[:, :, start:stop].reshape(n * ROWS, stop - start)
        slot = lax.broadcasted_iota(jnp.int32, (slots, n * ROWS), 0)
        place = lax.broadcasted_iota(jnp.int32, (slots, n * ROWS), 1)
        wanted = slot // SLOTS * ROWS + q * SLOTS + lax.rem(slot, SLOTS)
        pick = (place == wanted).astype(F32).astype(BF16)
        return jnp.dot(pick, rows, preferred_element_type=F32)

    for q in range(QUARTERS):
        normed_v[core, :, q * score_piece : (q + 1) * score_piece] = take(q, tail, end).astype(
            BF16
        )
    send(normed_v.at[core], normed_v.at[core], normed_sem.at[0], mate)
    digits = take(0, end, width)
    target = (digits[:, 0:1] * 256.0 + digits[:, 1:2]).astype(jnp.int32)
    for q in range(QUARTERS):
        x_ref[:, q * piece : (q + 1) * piece] = take(q, 0, piece).astype(BF16)
        u_ref[:, q * piece : (q + 1) * piece] = take(q, piece, tail).astype(BF16)

    def multiply(i, rows):
        loads[3 + i].wait()
        part_v[i] = lax.dot_general(
            rows[...], weight_v[i], (((1,), (1,)), ((), ())), preferred_element_type=F32
        )
        send(part_v.at[i], other_v.at[i], part_sem.at[i], mate)

    def summed(i):
        arrived(other_v.at[i], part_sem.at[i], mate)
        return part_v[i] + other_v[i]

    lane = lax.broadcasted_iota(jnp.int32, (slots, 128), 1)

    def pack(stats):
        return jnp.where(lane == 0, stats[0], jnp.where(lane == 1, stats[1], stats[2]))

    def combine(terms):
        peak = functools.reduce(jnp.maximum, [t[0] for t in terms])
        total = sum(t[1] * jnp.exp(t[0] - peak) for t in terms)
        return peak, total, sum(t[2] for t in terms)

    def split(packed):
        return packed[:, 0:1], packed[:, 1:2], packed[:, 2:3]

    stat_peers = [mate, x_peer, y_peer]

    def stat_send(i, stats):
        stat_v[i] = pack(stats)
        send(stat_v.at[i], stat_in.at[i], stat_sem.at[i], stat_peers[i])

    def stat_join(i, stats):
        arrived(stat_in.at[i], stat_sem.at[i], stat_peers[i])
        return combine([stats, split(stat_in[i])])

    multiply(0, x_ref)

    loads[6].wait()
    arrived(normed_v.at[1 - core], normed_sem.at[0], mate)
    vocab = head_v.shape[1]
    v_tile = 256

    @pl.loop(0, vocab // v_tile)
    def _(j):
        at_vocab = pl.ds(pl.multiple_of(j * v_tile, v_tile), v_tile)
        logits_v[:, at_vocab] = jnp.dot(
            normed_v[0], head_v[:score_half, at_vocab], preferred_element_type=F32
        ) + jnp.dot(normed_v[1], head_v[score_half:, at_vocab], preferred_element_type=F32)

    logits = logits_v[...]
    entry = lax.broadcasted_iota(jnp.int32, (slots, vocab), 1)
    hit = entry == target - (core * n + chip) * vocab
    peak = jnp.max(logits, axis=1, keepdims=True)
    total = jnp.sum(jnp.exp(logits - peak), axis=1, keepdims=True)
    wanted = jnp.sum(jnp.where(hit, logits, 0.0), axis=1, keepdims=True)
    stats = (peak, total, wanted)
    stat_send(0, stats)
    multiply(1, x_ref)
    stats = stat_join(0, stats)
    stat_send(1, stats)
    multiply(2, u_ref)
    stats = stat_join(1, stats)
    stat_send(2, stats)
    gate = summed(0)
    up = summed(1)
    s = jax.nn.sigmoid(gate)
    act = gate * s
    left_ref[2] = (act * up).astype(BF16)
    stats = stat_join(2, stats)
    stat_v[3] = pack(stats)
    for d in range(1, groups):
        send(stat_v.at[3], stat_in.at[2 + d], stat_sem.at[2 + d], z_to[d - 1])
    dhidden = summed(2)
    left_ref[0] = (dhidden * up * s * (1.0 + gate * (1.0 - s))).astype(BF16)
    left_ref[1] = (dhidden * act).astype(BF16)
    terms = [stats]
    for d in range(1, groups):
        source = (core, at(lax.rem(a + groups - d, groups), b, c))
        arrived(stat_in.at[2 + d], stat_sem.at[2 + d], source)
        terms.append(split(stat_in[2 + d]))
    peak, total, wanted = combine(terms)
    losses = peak + jnp.log(total) - wanted
    slot = lax.broadcasted_iota(jnp.int32, (slots, tokens), 0)
    mine = slot == place[0:1] + chip * SLOTS + core * CAP
    mine = mine & (jnp.broadcast_to(ranks_ref[...], (slots, tokens)) < keep_half)
    loss_ref[...] = jnp.sum(jnp.where(mine, losses, 0.0), axis=0, keepdims=True)
    for copy in sends:
        copy.wait_send()


def outer_kernel(left_ref, x_ref, u_ref, gate_ref, up_ref, down_ref):
    for i, (right, out) in enumerate([(x_ref, gate_ref), (x_ref, up_ref), (u_ref, down_ref)]):
        width = out.shape[1]
        step = 1024 if width % 1024 == 0 else width
        for k in range(width // step):
            out[:, k * step : (k + 1) * step] = lax.dot_general(
                left_ref[i],
                right[:, k * step : (k + 1) * step],
                (((0,), (0,)), ((), ())),
                preferred_element_type=F32,
            ).astype(BF16)


def on_device(
    scorer_hidden,
    scorer_gain,
    scorer_head,
    targets,
    ranks,
    train_input,
    cotangent,
    w_gate,
    w_up,
    w_down,
):
    n = lax.axis_size("fsdp")
    groups = n // 4
    slots = n * SLOTS
    score, vocab = scorer_head.shape
    units, half = w_gate.shape
    tokens = ranks.shape[0]
    width = 2 * half // QUARTERS + score // 2 // QUARTERS + 128
    vmem = pl.BlockSpec(memory_space=pltpu.VMEM)
    hbm = pl.BlockSpec(memory_space=pl.ANY)
    n_sends = 1 + (groups - 1) + 4 * groups + 1 + 3 + 3 + (groups - 1)
    dma = pltpu.SemaphoreType.DMA
    loss, left, inputs, upstream = pl.pallas_call(
        functools.partial(exchange_kernel, n),
        out_shape=(
            jax.ShapeDtypeStruct((1, tokens), F32),
            jax.ShapeDtypeStruct((3, slots, units), BF16),
            jax.ShapeDtypeStruct((slots, half), BF16),
            jax.ShapeDtypeStruct((slots, half), BF16),
        ),
        in_specs=[vmem] * 3 + [hbm] * 7,
        out_specs=(vmem,) * 4,
        scratch_shapes=[
            pltpu.VMEM(scorer_hidden.shape, BF16),
            pltpu.VMEM(train_input.shape, BF16),
            pltpu.VMEM(cotangent.shape, BF16),
            pltpu.VMEM((3, units, half), BF16),
            pltpu.VMEM((score, vocab), BF16),
            pltpu.VMEM((2, ROWS, width), BF16),
            pltpu.VMEM((ROWS, width), BF16),
            pltpu.VMEM((n, ROWS, width), BF16),
            pltpu.VMEM((2, slots, score // 2), BF16),
            pltpu.VMEM((3, slots, units), F32),
            pltpu.VMEM((3, slots, units), F32),
            pltpu.VMEM((slots, vocab), F32),
            pltpu.VMEM((4, slots, 128), F32),
            pltpu.VMEM((2 + groups, slots, 128), F32),
            dma((7,)),
            dma((n_sends,)),
            dma((1,)),
            dma((5, groups)),
            dma((1,)),
            dma((3,)),
            dma((2 + groups,)),
        ],
        compiler_params=pltpu.CompilerParams(
            collective_id=0, has_side_effects=True, vmem_limit_bytes=60 * 2**20
        ),
    )(
        scorer_gain.reshape(1, score),
        targets.reshape(1, tokens),
        ranks.reshape(1, tokens),
        scorer_hidden,
        train_input,
        cotangent,
        w_gate,
        w_up,
        w_down,
        scorer_head,
    )
    tile = 128 if units % 128 == 0 else units
    whole = pl.BlockSpec((slots, half), lambda i: (0, 0))
    out = pl.BlockSpec((tile, half), lambda i: (i, 0))
    grads = pl.pallas_call(
        outer_kernel,
        grid=(units // tile,),
        out_shape=(jax.ShapeDtypeStruct((units, half), BF16),) * 3,
        in_specs=[pl.BlockSpec((3, slots, tile), lambda i: (0, 0, i)), whole, whole],
        out_specs=(out,) * 3,
        compiler_params=pltpu.CompilerParams(vmem_limit_bytes=60 * 2**20),
    )(left, inputs, upstream)
    return (loss.reshape(tokens),) + tuple(grads)


def solution(mesh):
    in_specs = (
        P(("grp", "fsdp"), None),
        P(),
        P(None, ("grp", "fsdp")),
        P(("grp", "fsdp")),
        P(("grp", "fsdp")),
        P(("grp", "fsdp"), None),
        P(("grp", "fsdp"), None),
        P("fsdp", "grp"),
        P("fsdp", "grp"),
        P("fsdp", "grp"),
    )
    out_specs = (P(("grp", "fsdp")), P("fsdp", "grp"), P("fsdp", "grp"), P("fsdp", "grp"))
    return jax.shard_map(
        on_device, mesh=mesh, in_specs=in_specs, out_specs=out_specs, check_vma=False
    )
```
